32 devices in a mesh: region: 16 (over z, y, core), obs: 2 (over x).
Axes of the slice: x: 2, y: 2, z: 4, core: 2. Of those that a mesh axis runs over, the one named last changes fastest.
Arguments:
- obs_anomaly: bfloat16 [512, 2048, 128], P('region', 'obs'), may hold values from -1.5 to 1.5
- innovation: bfloat16 [512, 2048], P('region', 'obs'), may hold values from -6 to 6
- obs_count: int32 [512], P('region'), may hold values from 512 to 2048, as said below
- neighbour: int32 [512, 5], P('region'), may hold values from 0 to 511, as said below
- taper: float32 [512, 5], P('region'), may hold values from 0.1 to 1
- param_anomaly: bfloat16 [512, 1024, 128], P('region', 'obs'), may hold values from -6 to 6
- param_mean: float32 [512, 1024], P('region', 'obs'), may hold values from -6 to 6
Outputs:
- analysis: bfloat16 [512, 1024, 128], P('region', 'obs')
The draws below stay inside these ranges and needn't reach their ends.
Inputs may be any that keep to these rules, and one draw needn't show every extreme that they name: `obs_count`: region 512 counts: some region has all 2048 slots live. neighbour[g, 0] = g; every other entry differs from g cyclically by 1 to 32 regions.
All inputs are finite; a program needn't handle non-finite values.
Results may differ from the reference program's by a relative error of at most 0.013.
Values may be sent and summed in bfloat16 or wider, within the bound.
A program may use at most 192 MiB of HBM per device.

```python
import jax
import jax.numpy as jnp
from jax import lax

MEMBERS = 128
NB = 5
R_DEV = 32
OBS_REG = 2048
PAR_REG = 1024
NREG = 512
N_REGION = 16


def draw_obs_anomaly(key, part):
    key = jax.random.fold_in(key, 37)
    key_noise, key_dir, key_coef = jax.random.split(key, 3)
    noise = jax.random.truncated_normal(key_noise, -4.0, 4.0, (NREG, OBS_REG, MEMBERS), jnp.float32)
    direction = jax.random.truncated_normal(key_dir, -2.5, 2.5, (NREG, 1, MEMBERS), jnp.float32)
    amplitude = 0.1
    coefs = jax.random.truncated_normal(key_coef, -2.5, 2.5, (NREG, OBS_REG, 1), jnp.float32)
    values = 0.2 * noise + amplitude * coefs * direction
    return values.astype(jnp.bfloat16)


def draw_obs_count(key, part):
    key = jax.random.fold_in(key, 11)
    key_one, key_two, key_three = jax.random.split(key, 3)
    first = jax.random.randint(key_one, (NREG,), OBS_REG // 4, OBS_REG + 1)
    second = jax.random.randint(key_two, (NREG,), OBS_REG // 4, OBS_REG + 1)
    counts = jnp.minimum(first, second)
    target = jax.random.randint(key_three, (), 0, NREG)
    counts = jnp.where(jnp.arange(NREG) == target, OBS_REG, counts)
    return counts.astype(jnp.int32)


def draw_neighbour(key, part):
    key = jax.random.fold_in(key, 23)
    offsets = jax.random.randint(key, (NREG, NB - 1), 1, R_DEV + 1)
    signs = jnp.where(jnp.arange(NB - 1) % 2 == 0, 1, -1)
    own = jnp.arange(NREG, dtype=jnp.int32)
    others = (own[:, None] + signs[None, :] * offsets) % NREG
    return jnp.concatenate([own[:, None], others], axis=1).astype(jnp.int32)


def levels(stream_key, shape, pieces, low, high):
    loudness, own = 1.0, jax.random.fold_in(stream_key, 6)
    for position, parts in pieces:
        draws = jnp.exp(jax.random.uniform(jax.random.fold_in(own, position), (parts,), jnp.float32, low / len(pieces), high / len(pieces)))
        loudness = loudness * jnp.repeat(draws, shape[position] // parts).reshape([-1 if axis == position else 1 for axis in range(len(shape))])
    return loudness


def gaussian(rng, extent, scale, reach, shards=(), held_as=jnp.bfloat16):
    result = scale * jax.random.normal(rng, extent, jnp.float32)
    if shards:
        result = result * levels(rng, extent, shards, -0.22, 0.18)
    return jnp.clip(result, -reach, reach).astype(held_as)


def setup_inputs(seed: int = 0) -> dict:
    key_of = jax.random.split(jax.random.key(seed), 8)
    return {
        "obs_anomaly": draw_obs_anomaly(jax.random.fold_in(key_of[7], 71), 0),
        "innovation": gaussian(key_of[1], (NREG, OBS_REG), 1.0, 6.0, ((0, 16), (1, 2))),
        "obs_count": draw_obs_count(jax.random.fold_in(key_of[7], 71), 0),
        "neighbour": draw_neighbour(jax.random.fold_in(key_of[7], 71), 0),
        "taper": jnp.clip(0.1 + 0.9 * jax.random.uniform(key_of[4], (NREG, NB), jnp.float32) ** levels(key_of[4], (NREG, NB), ((0, 16),), -0.2, 0.2), 0.1, 1.0),
        "param_anomaly": gaussian(key_of[5], (NREG, PAR_REG, MEMBERS), 1.0, 6.0, ((0, 16), (1, 2))),
        "param_mean": gaussian(key_of[6], (NREG, PAR_REG), 1.0, 6.0, ((0, 16), (1, 2)), jnp.float32),
    }


def lower_inverse(lower):
    width = lower.shape[-1]
    rows = jnp.arange(width, dtype=jnp.int32)[:, None]
    cols = jnp.arange(width, dtype=jnp.int32)[None, :]
    diag = jnp.diagonal(lower, axis1=-2, axis2=-1)
    inverse = jnp.where(rows == cols, (1.0 / diag)[..., None, :], jnp.zeros((), jnp.float32))
    block = 1
    while block < width:
        row_block = rows // block
        col_block = cols // block
        keep = (row_block % 2 == 1) & (col_block == row_block - 1)
        corner = jnp.where(keep, lower, jnp.zeros((), jnp.float32))
        inner = jnp.einsum('bij,bjk->bik', corner, inverse, precision=lax.Precision.HIGHEST)
        inverse = inverse - jnp.einsum('bij,bjk->bik', inverse, inner, precision=lax.Precision.HIGHEST)
        block = block * 2
    return inverse

def solve_region(local_gram, local_proj):
    width = local_gram.shape[-1]
    eye = jnp.eye(width, dtype=jnp.float32)
    precision_mat = (width - 1.0) * eye + local_gram
    lower = jnp.linalg.cholesky(precision_mat)
    inverse_lower = lower_inverse(lower)
    step_one = jnp.einsum('bij,bj->bi', inverse_lower, local_proj, precision=lax.Precision.HIGHEST)
    mean_weight = jnp.einsum('bji,bj->bi', inverse_lower, step_one, precision=lax.Precision.HIGHEST)
    spread = jnp.sqrt(width - 1.0) * jnp.swapaxes(inverse_lower, -1, -2)
    return (mean_weight[..., None] + spread).astype(jnp.bfloat16)

def reference(obs_anomaly, innovation, obs_count, neighbour, taper, param_anomaly, param_mean):
    slots = jnp.arange(OBS_REG, dtype=jnp.int32)
    live = slots[None, :] < obs_count[:, None]
    masked_y = jnp.where(live[..., None], obs_anomaly, jnp.zeros((), jnp.bfloat16))
    masked_d = jnp.where(live, innovation, jnp.zeros((), jnp.bfloat16))
    blocks_y = masked_y.reshape(N_REGION, R_DEV, OBS_REG, MEMBERS)
    blocks_d = masked_d.reshape(N_REGION, R_DEV, OBS_REG)

    def grams_of(pair):
        ys, ds = pair
        yf = ys.astype(jnp.float32)
        gram = jnp.einsum('roi,roj->rij', yf, yf, precision=lax.Precision.HIGHEST)
        proj = jnp.einsum('roi,ro->ri', yf, ds.astype(jnp.float32), precision=lax.Precision.HIGHEST)
        return (gram, proj)
    gram, proj = lax.map(grams_of, (blocks_y, blocks_d))
    gram = gram.reshape(NREG, MEMBERS, MEMBERS)
    proj = proj.reshape(NREG, MEMBERS)

    def combine(pair):
        idx, wts = pair
        local_gram = jnp.einsum('rk,rkij->rij', wts, gram[idx], precision=lax.Precision.HIGHEST)
        local_proj = jnp.einsum('rk,rki->ri', wts, proj[idx], precision=lax.Precision.HIGHEST)
        return solve_region(local_gram, local_proj)
    transform = lax.map(combine, (neighbour.reshape(N_REGION, R_DEV, NB), taper.reshape(N_REGION, R_DEV, NB)))
    transform = transform.reshape(NREG, MEMBERS, MEMBERS)
    moved = jnp.einsum('rpk,rkj->rpj', param_anomaly.astype(jnp.float32), transform.astype(jnp.float32), precision=lax.Precision.HIGHEST)
    return (param_mean[..., None] + moved).astype(jnp.bfloat16)
```

```python
import functools

import jax
import jax.numpy as jnp
from jax import lax
from jax.experimental import pallas as pl
from jax.experimental.pallas import tpu as pltpu
from jax.sharding import PartitionSpec as P

MESH = pl.DeviceIdType.MESH
MEMBERS = 128
ROWS = MEMBERS + 16
PANEL = 16
LAG = 3
F32 = jnp.float32
BF16 = jnp.bfloat16


def dot_rows(left, right):
    return lax.dot_general(left, right, (((0,), (0,)), ((), ())), preferred_element_type=F32)


def iotas(shape):
    row = lax.broadcasted_iota(jnp.int32, shape, len(shape) - 2)
    col = lax.broadcasted_iota(jnp.int32, shape, len(shape) - 1)
    return row, col


def gram_kernel(
    n_region, y_hbm, d_ref, count_ref, gath, ybuf, dbuf, part, recv,
    y_sem, xs_sem, xr_sem, ups_sem, upr_sem, dns_sem, dnr_sem,
):
    pairs, _, slots, _ = ybuf.shape
    x = lax.axis_index("obs")
    me = lax.axis_index("region")
    partner = {"obs": 1 - x}
    right = {"region": lax.rem(me + 1, n_region)}
    left = {"region": lax.rem(me + n_region - 1, n_region)}

    def fetch(p):
        return pltpu.make_async_copy(y_hbm.at[pl.ds(2 * p, 2)], ybuf.at[p], y_sem.at[p])

    def swap(p):
        return pltpu.make_async_remote_copy(
            src_ref=part.at[p], dst_ref=recv.at[p], send_sem=xs_sem.at[p], recv_sem=xr_sem.at[p],
            device_id=partner, device_id_type=MESH,
        )

    def up(q):
        return pltpu.make_async_remote_copy(
            src_ref=gath.at[pairs + q], dst_ref=gath.at[q], send_sem=ups_sem.at[q],
            recv_sem=upr_sem.at[q], device_id=right, device_id_type=MESH,
        )

    def down(q):
        return pltpu.make_async_remote_copy(
            src_ref=gath.at[pairs + q], dst_ref=gath.at[2 * pairs + q], send_sem=dns_sem.at[q],
            recv_sem=dnr_sem.at[q], device_id=left, device_id_type=MESH,
        )

    def each(first, last, step):
        lax.fori_loop(first, last, lambda i, c: (step(i), c)[1], 0)

    each(0, pairs, lambda p: fetch(p).start())
    barrier = pltpu.get_barrier_semaphore()
    for other in (partner, left, right):
        pl.semaphore_signal(barrier, inc=1, device_id=other, device_id_type=MESH)
    dbuf[...] = d_ref[...].astype(F32)
    pl.semaphore_wait(barrier, 3)

    row, col = iotas((MEMBERS, MEMBERS))
    ext_row, _ = iotas((ROWS - MEMBERS, MEMBERS))
    slot_row, _ = iotas((slots, MEMBERS))
    slot_lane = lax.broadcasted_iota(jnp.int32, (1, slots), 1)

    def grams(p):
        fetch(p).wait()
        found = []
        for i in range(2):
            live = count_ref[2 * p + i] - x * slots
            y = ybuf[p, i]
            masked = jnp.where(slot_row < live, y, jnp.zeros((), BF16))
            d = jnp.where(slot_lane < live, dbuf[pl.ds(2 * p + i, 1), :], 0.0).astype(BF16)
            found.append((dot_rows(masked, y), jnp.dot(d, y, preferred_element_type=F32)))
        (gram0, proj0), (gram1, proj1) = found
        part[p, :MEMBERS] = jnp.where(row <= col, gram0, gram1).astype(BF16)
        diag = jnp.sum(jnp.where(row == col, gram1, 0.0), axis=0, keepdims=True)
        ext = jnp.where(ext_row == 0, diag, jnp.where(ext_row == 1, proj0, jnp.where(ext_row == 2, proj1, 0.0)))
        part[p, MEMBERS:] = ext.astype(BF16)
        swap(p).start()

    def forward(q):
        swap(q).wait_recv()
        gath[pairs + q] = (part[q].astype(F32) + recv[q].astype(F32)).astype(BF16)
        up(q).start()
        down(q).start()

    each(0, LAG, grams)

    def both(p):
        grams(p)
        forward(p - LAG)

    each(LAG, pairs, both)
    each(pairs - LAG, pairs, forward)

    def finish(q):
        swap(q).wait_send()
        up(q).wait()
        down(q).wait()

    each(0, pairs, finish)


def solve_kernel(
    place_ref, taper_ref, gath, par_hbm, mean_ref, out_hbm, mat, proj, pmt, parbuf, outbuf, in_sem, out_sem
):
    regions = mat.shape[0]
    near = taper_ref.shape[0] // regions

    def fetch(g):
        return pltpu.make_async_copy(par_hbm.at[g], parbuf.at[g], in_sem.at[g])

    def put(g):
        return pltpu.make_async_copy(outbuf.at[g], out_hbm.at[g], out_sem.at[g])

    def each(first, last, step, unroll=1):
        lax.fori_loop(first, last, lambda i, c: (step(i), c)[1], 0, unroll=unroll)

    each(0, regions, lambda g: fetch(g).start())

    pm = mean_ref[...]
    high = pm.astype(BF16).astype(F32)
    mid = (pm - high).astype(BF16).astype(F32)
    low = pm - high - mid
    pad = jnp.zeros((MEMBERS - 3 * regions, pm.shape[1]), F32)
    pmt[...] = jnp.concatenate([high, mid, low, pad], axis=0).T.astype(BF16)

    row, col = iotas((MEMBERS, MEMBERS))
    upper = row <= col
    diagonal = row == col

    def combine(g):
        acc = jnp.zeros((MEMBERS, MEMBERS), F32)
        ext = jnp.zeros((ROWS - MEMBERS, MEMBERS), F32)
        ext_row, _ = iotas((ROWS - MEMBERS, MEMBERS))
        for k in range(near):
            place = place_ref[g * near + k]
            weight = taper_ref[g * near + k]
            odd = place % 2
            even_w = jnp.where(odd == 0, weight, 0.0)
            odd_w = jnp.where(odd == 0, 0.0, weight)
            tile = gath[place // 2].astype(F32)
            acc = acc + jnp.where(upper, even_w, odd_w) * tile[:MEMBERS]
            ext = ext + jnp.where(ext_row == 1, even_w, odd_w) * tile[MEMBERS:]
        other = jnp.where(diagonal, ext[0:1] + (MEMBERS - 1.0), acc.T)
        mat[g] = acc + other
        proj[g] = jnp.broadcast_to(ext[1:2] + ext[2:3], (8, MEMBERS))

    each(0, regions, combine, 2)

    half = PANEL // 2
    h_row, h_lane = iotas((regions, half, MEMBERS))
    p_row, p_lane = iotas((PANEL, MEMBERS))

    def panel(p):
        start = pl.multiple_of(p * PANEL, PANEL)
        slab = mat[:, pl.ds(start, PANEL), :].reshape(regions * PANEL, MEMBERS)
        slab = pltpu.roll(slab, lax.rem(MEMBERS - start, MEMBERS), 1).reshape(regions, PANEL, MEMBERS)
        top, bot = slab[:, :half], slab[:, half:]
        inv_top = jnp.zeros((regions, half, MEMBERS), F32)
        inv_bot = jnp.zeros((regions, half, MEMBERS), F32)

        def shape(a):
            return jnp.broadcast_to(a, (regions, half, MEMBERS))

        for j in range(PANEL):
            i = j % half
            source = top if j < half else bot
            col_s = shape(source[:, :, j : j + 1])
            inv = 1.0 / shape(col_s[:, i : i + 1])
            pivot = jnp.where(h_lane == j, 1.0, shape(source[:, i : i + 1]))
            scaled = inv * pivot
            if j < half:
                inv_top = jnp.where(h_row == i, inv, inv_top)
                col_b = shape(bot[:, :, j : j + 1])
                below = h_row > i
                top = jnp.where((h_lane == j) & below, 0.0, top) - jnp.where(below, col_s, 0.0) * scaled
                bot = jnp.where(h_lane == j, 0.0, bot) - col_b * scaled
            else:
                inv_bot = jnp.where(h_row == i, inv, inv_bot)
                below = h_row > i
                bot = jnp.where((h_lane == j) & below, 0.0, bot) - jnp.where(below, col_s, 0.0) * scaled

        slab = jnp.concatenate([top, bot], axis=1)
        inv = jnp.concatenate([inv_top, inv_bot], axis=1)
        slab = pltpu.roll(slab.reshape(regions * PANEL, MEMBERS), start, 1).reshape(regions, PANEL, MEMBERS)
        mat[:, pl.ds(start, PANEL), :] = slab
        later = p_lane >= start + PANEL
        own = (p_lane >= start) & (p_lane < start + PANEL)
        strict = own & (p_lane - start > p_row)
        on_diag = own & (p_lane - start == p_row)
        clear = (row >= start + PANEL) & (col >= start) & (col < start + PANEL)
        for g in range(regions):
            factor = jnp.where(later, slab[g] * inv[g], 0.0)
            full = jnp.where(on_diag, 1.0, jnp.where(strict, 0.0, slab[g]))
            factor_h = factor.astype(BF16)
            factor_l = (factor - factor_h.astype(F32)).astype(BF16)
            full_h = full.astype(BF16)
            full_l = (full - full_h.astype(F32)).astype(BF16)
            update = dot_rows(
                jnp.concatenate([factor_h, factor_h, factor_l], axis=0),
                jnp.concatenate([full_h, full_l, full_h], axis=0),
            )
            mat[g] = jnp.where(clear, 0.0, mat[g]) - update

    each(0, MEMBERS // PANEL, panel)

    def apply(g):
        a = mat[g]
        pivots = jnp.sum(jnp.where(diagonal, a, 0.0), axis=1, keepdims=True)
        inverse = lax.rsqrt(pivots) * jnp.where(diagonal, 1.0, jnp.where(row > col, a, 0.0))
        step = jnp.sum(inverse * proj[g, 0:1, :], axis=1, keepdims=True)
        mean_weight = jnp.sum(inverse * step, axis=0, keepdims=True)
        transform = (mean_weight + (MEMBERS - 1.0) ** 0.5 * inverse).astype(BF16)
        pick = (col == g) | (col == regions + g) | (col == 2 * regions + g)
        ones = jnp.where(pick, 1.0, 0.0).astype(BF16)
        fetch(g).wait()
        moved = lax.dot_general(
            jnp.concatenate([parbuf[g], pmt[...]], axis=1),
            jnp.concatenate([transform, ones], axis=1),
            (((1,), (1,)), ((), ())),
            preferred_element_type=F32,
        )
        outbuf[g] = moved.astype(BF16)
        put(g).start()

    each(0, regions, apply, 2)
    each(0, regions, lambda g: put(g).wait())


def body(n_region, obs_anomaly, innovation, obs_count, neighbour, taper, param_anomaly, param_mean):
    regions, slots, _ = obs_anomaly.shape
    pars = param_anomaly.shape[1]
    pairs = regions // 2
    vmem = pl.BlockSpec(memory_space=pltpu.VMEM)
    smem = pl.BlockSpec(memory_space=pltpu.SMEM)
    hbm = pl.BlockSpec(memory_space=pl.ANY)
    gath = pl.pallas_call(
        functools.partial(gram_kernel, n_region),
        out_shape=jax.ShapeDtypeStruct((3 * pairs, ROWS, MEMBERS), BF16),
        in_specs=[hbm, vmem, smem],
        out_specs=vmem,
        scratch_shapes=[
            pltpu.VMEM((pairs, 2, slots, MEMBERS), BF16),
            pltpu.VMEM((regions, slots), F32),
            pltpu.VMEM((pairs, ROWS, MEMBERS), BF16),
            pltpu.VMEM((pairs, ROWS, MEMBERS), BF16),
        ]
        + [pltpu.SemaphoreType.DMA((pairs,))] * 7,
        compiler_params=pltpu.CompilerParams(
            collective_id=0, has_side_effects=True, vmem_limit_bytes=40 * 2**20
        ),
    )(obs_anomaly, innovation, obs_count)

    total = regions * n_region
    first = lax.axis_index("region") * regions
    place = (neighbour - first + regions) % total
    return pl.pallas_call(
        solve_kernel,
        out_shape=jax.ShapeDtypeStruct((regions, pars, MEMBERS), BF16),
        in_specs=[smem, smem, vmem, hbm, vmem],
        out_specs=hbm,
        scratch_shapes=[
            pltpu.VMEM((regions, MEMBERS, MEMBERS), F32),
            pltpu.VMEM((regions, 8, MEMBERS), F32),
            pltpu.VMEM((pars, MEMBERS), BF16),
            pltpu.VMEM((regions, pars, MEMBERS), BF16),
            pltpu.VMEM((regions, pars, MEMBERS), BF16),
            pltpu.SemaphoreType.DMA((regions,)),
            pltpu.SemaphoreType.DMA((regions,)),
        ],
        compiler_params=pltpu.CompilerParams(vmem_limit_bytes=40 * 2**20),
    )(place.reshape(-1), taper.reshape(-1), gath, param_anomaly, param_mean)


def solution(mesh):
    in_specs = (
        P("region", "obs", None),
        P("region", "obs"),
        P("region"),
        P("region", None),
        P("region", None),
        P("region", "obs", None),
        P("region", "obs"),
    )
    out_specs = P("region", "obs", None)
    return jax.shard_map(
        functools.partial(body, mesh.shape["region"]),
        mesh=mesh, in_specs=in_specs, out_specs=out_specs, check_vma=False,
    )
```

```python
import functools

import jax
import jax.numpy as jnp
from jax import lax
from jax.experimental import pallas as pl
from jax.experimental.pallas import tpu as pltpu
from jax.sharding import PartitionSpec as P

MESH = pl.DeviceIdType.MESH
MEMBERS = 128
ROWS = MEMBERS + 16
PANEL = 8
LAG = 3
F32 = jnp.float32
BF16 = jnp.bfloat16


def dot_rows(left, right):
    return lax.dot_general(left, right, (((0,), (0,)), ((), ())), preferred_element_type=F32)


def iotas(shape):
    row = lax.broadcasted_iota(jnp.int32, shape, len(shape) - 2)
    col = lax.broadcasted_iota(jnp.int32, shape, len(shape) - 1)
    return row, col


def gram_kernel(
    n_region, y_hbm, d_ref, count_ref, gath, ybuf, dbuf, part, recv,
    y_sem, xs_sem, xr_sem, ups_sem, upr_sem, dns_sem, dnr_sem,
):
    pairs, _, slots, _ = ybuf.shape
    x = lax.axis_index("obs")
    me = lax.axis_index("region")
    partner = {"obs": 1 - x}
    right = {"region": lax.rem(me + 1, n_region)}
    left = {"region": lax.rem(me + n_region - 1, n_region)}

    def fetch(p):
        return pltpu.make_async_copy(y_hbm.at[pl.ds(2 * p, 2)], ybuf.at[p], y_sem.at[p])

    def swap(p):
        return pltpu.make_async_remote_copy(
            src_ref=part.at[p], dst_ref=recv.at[p], send_sem=xs_sem.at[p], recv_sem=xr_sem.at[p],
            device_id=partner, device_id_type=MESH,
        )

    def up(q):
        return pltpu.make_async_remote_copy(
            src_ref=gath.at[pairs + q], dst_ref=gath.at[q], send_sem=ups_sem.at[q],
            recv_sem=upr_sem.at[q], device_id=right, device_id_type=MESH,
        )

    def down(q):
        return pltpu.make_async_remote_copy(
            src_ref=gath.at[pairs + q], dst_ref=gath.at[2 * pairs + q], send_sem=dns_sem.at[q],
            recv_sem=dnr_sem.at[q], device_id=left, device_id_type=MESH,
        )

    def each(first, last, step):
        lax.fori_loop(first, last, lambda i, c: (step(i), c)[1], 0)

    each(0, pairs, lambda p: fetch(p).start())
    barrier = pltpu.get_barrier_semaphore()
    for other in (partner, left, right):
        pl.semaphore_signal(barrier, inc=1, device_id=other, device_id_type=MESH)
    dbuf[...] = d_ref[...].astype(F32)
    pl.semaphore_wait(barrier, 3)

    row, col = iotas((MEMBERS, MEMBERS))
    ext_row, _ = iotas((ROWS - MEMBERS, MEMBERS))
    slot_row, _ = iotas((slots, MEMBERS))
    slot_lane = lax.broadcasted_iota(jnp.int32, (1, slots), 1)

    def grams(p):
        fetch(p).wait()
        found = []
        for i in range(2):
            live = count_ref[2 * p + i] - x * slots
            y = ybuf[p, i]
            masked = jnp.where(slot_row < live, y, jnp.zeros((), BF16))
            d = jnp.where(slot_lane < live, dbuf[pl.ds(2 * p + i, 1), :], 0.0).astype(BF16)
            found.append((dot_rows(masked, y), jnp.dot(d, y, preferred_element_type=F32)))
        (gram0, proj0), (gram1, proj1) = found
        part[p, :MEMBERS] = jnp.where(row <= col, gram0, gram1).astype(BF16)
        diag = jnp.sum(jnp.where(row == col, gram1, 0.0), axis=0, keepdims=True)
        ext = jnp.where(ext_row == 0, diag, jnp.where(ext_row == 1, proj0, jnp.where(ext_row == 2, proj1, 0.0)))
        part[p, MEMBERS:] = ext.astype(BF16)
        swap(p).start()

    def forward(q):
        swap(q).wait_recv()
        gath[pairs + q] = (part[q].astype(F32) + recv[q].astype(F32)).astype(BF16)
        up(q).start()
        down(q).start()

    each(0, LAG, grams)

    def both(p):
        grams(p)
        forward(p - LAG)

    each(LAG, pairs, both)
    each(pairs - LAG, pairs, forward)

    def finish(q):
        swap(q).wait_send()
        up(q).wait()
        down(q).wait()

    each(0, pairs, finish)


def solve_kernel(
    total, near_ref, taper_ref, gath, par_hbm, mean_ref, out_hbm, mat, proj, pmt, parbuf, outbuf, in_sem, out_sem
):
    regions = mat.shape[0]
    near = taper_ref.shape[0]
    before = total + regions - lax.axis_index("region") * regions

    def fetch(g):
        return pltpu.make_async_copy(par_hbm.at[g], parbuf.at[g], in_sem.at[g])

    def put(g):
        return pltpu.make_async_copy(outbuf.at[g], out_hbm.at[g], out_sem.at[g])

    def each(first, last, step, unroll=1):
        lax.fori_loop(first, last, lambda i, c: (step(i), c)[1], 0, unroll=unroll)

    each(0, regions, lambda g: fetch(g).start())

    pm = mean_ref[...]
    high = pm.astype(BF16).astype(F32)
    mid = (pm - high).astype(BF16).astype(F32)
    low = pm - high - mid
    pad = jnp.zeros((MEMBERS - 3 * regions, pm.shape[1]), F32)
    pmt[...] = jnp.concatenate([high, mid, low, pad], axis=0).T.astype(BF16)

    row, col = iotas((MEMBERS, MEMBERS))
    upper = row <= col
    diagonal = row == col

    def combine(g):
        acc = jnp.zeros((MEMBERS, MEMBERS), F32)
        ext = jnp.zeros((ROWS - MEMBERS, MEMBERS), F32)
        ext_row, _ = iotas((ROWS - MEMBERS, MEMBERS))
        for k in range(near):
            place = lax.rem(near_ref[k, g] + before, total)
            weight = taper_ref[k, g]
            odd = place % 2
            even_w = jnp.where(odd == 0, weight, 0.0)
            odd_w = jnp.where(odd == 0, 0.0, weight)
            tile = gath[place // 2].astype(F32)
            acc = acc + jnp.where(upper, even_w, odd_w) * tile[:MEMBERS]
            ext = ext + jnp.where(ext_row == 1, even_w, odd_w) * tile[MEMBERS:]
        other = jnp.where(diagonal, ext[0:1] + (MEMBERS - 1.0), acc.T)
        mat[g] = acc + other
        proj[g] = jnp.broadcast_to(ext[1:2] + ext[2:3], (8, MEMBERS))

    each(0, regions, combine, 2)

    h_row, h_lane = iotas((regions, PANEL, MEMBERS))
    p_row, p_lane = iotas((PANEL, MEMBERS))

    def shape(a):
        return jnp.broadcast_to(a, (regions, PANEL, MEMBERS))

    def panel(base, p):
        start = pl.multiple_of(p * PANEL, PANEL)
        slab = mat[:, pl.ds(start, PANEL), :].reshape(regions * PANEL, MEMBERS)
        slab = pltpu.roll(slab, lax.rem(MEMBERS - start, MEMBERS), 1).reshape(regions, PANEL, MEMBERS)
        for j in range(PANEL):
            col_j = shape(slab[:, :, j : j + 1])
            root = lax.rsqrt(shape(col_j[:, j : j + 1]))
            pivot = jnp.where(h_lane == j, 1.0, shape(slab[:, j : j + 1])) * root
            factor = jnp.where(h_row > j, col_j * root, jnp.where(h_row == j, -1.0, 0.0))
            drop = (h_row == j) | ((h_lane == j) & (h_row > j))
            slab = jnp.where(drop, 0.0, slab) - factor * pivot
        slab = pltpu.roll(slab.reshape(regions * PANEL, MEMBERS), start, 1).reshape(regions, PANEL, MEMBERS)
        mat[:, pl.ds(start, PANEL), :] = slab
        later = p_lane >= start + PANEL
        strict = (p_lane < start + PANEL) & (p_lane - start > p_row)
        clear = (row[base:] >= start + PANEL) & (col[base:] >= start) & (col[base:] < start + PANEL)
        for g in range(regions):
            full = jnp.where(strict, 0.0, slab[g])
            full_h = full.astype(BF16).astype(F32)
            full_l = full - full_h
            factor_h = jnp.where(later, full_h, 0.0)
            factor_l = jnp.where(later, full_l, 0.0)
            update = dot_rows(
                jnp.concatenate([factor_h, factor_h, factor_l, factor_l], axis=0).astype(BF16),
                jnp.concatenate([full_h, full_l, full_h, full_l], axis=0).astype(BF16),
            )
            mat[g, base:] = jnp.where(clear, 0.0, mat[g, base:]) - update[base:]

    steps = MEMBERS // PANEL
    parts = 4
    for part in range(parts):
        first, last = part * steps // parts, (part + 1) * steps // parts
        each(first, last, functools.partial(panel, first * PANEL))

    def apply(g):
        inverse = jnp.where(row >= col, mat[g], 0.0)
        step = jnp.sum(inverse * proj[g, 0:1, :], axis=1, keepdims=True)
        mean_weight = jnp.sum(inverse * step, axis=0, keepdims=True)
        transform = (mean_weight + (MEMBERS - 1.0) ** 0.5 * inverse).astype(BF16)
        pick = (col == g) | (col == regions + g) | (col == 2 * regions + g)
        ones = jnp.where(pick, 1.0, 0.0).astype(BF16)
        fetch(g).wait()
        moved = lax.dot_general(
            jnp.concatenate([parbuf[g], pmt[...]], axis=1),
            jnp.concatenate([transform, ones], axis=1),
            (((1,), (1,)), ((), ())),
            preferred_element_type=F32,
        )
        outbuf[g] = moved.astype(BF16)
        put(g).start()

    each(0, regions, apply, 4)
    each(0, regions, lambda g: put(g).wait())


def body(n_region, obs_anomaly, innovation, obs_count, neighbour, taper, param_anomaly, param_mean):
    regions, slots, _ = obs_anomaly.shape
    pars = param_anomaly.shape[1]
    pairs = regions // 2
    vmem = pl.BlockSpec(memory_space=pltpu.VMEM)
    smem = pl.BlockSpec(memory_space=pltpu.SMEM)
    hbm = pl.BlockSpec(memory_space=pltpu.HBM)
    gath = pl.pallas_call(
        functools.partial(gram_kernel, n_region),
        out_shape=jax.ShapeDtypeStruct((3 * pairs, ROWS, MEMBERS), BF16),
        in_specs=[hbm, vmem, smem],
        out_specs=vmem,
        scratch_shapes=[
            pltpu.VMEM((pairs, 2, slots, MEMBERS), BF16),
            pltpu.VMEM((regions, slots), F32),
            pltpu.VMEM((pairs, ROWS, MEMBERS), BF16),
            pltpu.VMEM((pairs, ROWS, MEMBERS), BF16),
        ]
        + [pltpu.SemaphoreType.DMA((pairs,))] * 7,
        compiler_params=pltpu.CompilerParams(
            collective_id=0, has_side_effects=True, vmem_limit_bytes=40 * 2**20
        ),
    )(obs_anomaly, innovation, obs_count)

    return pl.pallas_call(
        functools.partial(solve_kernel, regions * n_region),
        out_shape=jax.ShapeDtypeStruct((regions, pars, MEMBERS), BF16),
        in_specs=[smem, smem, vmem, hbm, vmem],
        out_specs=hbm,
        scratch_shapes=[
            pltpu.VMEM((regions, MEMBERS, MEMBERS), F32),
            pltpu.VMEM((regions, 8, MEMBERS), F32),
            pltpu.VMEM((pars, MEMBERS), BF16),
            pltpu.VMEM((regions, pars, MEMBERS), BF16),
            pltpu.VMEM((regions, pars, MEMBERS), BF16),
            pltpu.SemaphoreType.DMA((regions,)),
            pltpu.SemaphoreType.DMA((regions,)),
        ],
        compiler_params=pltpu.CompilerParams(vmem_limit_bytes=40 * 2**20),
    )(neighbour.T, taper.T, gath, param_anomaly, param_mean)


def solution(mesh):
    in_specs = (
        P("region", "obs", None),
        P("region", "obs"),
        P("region"),
        P("region", None),
        P("region", None),
        P("region", "obs", None),
        P("region", "obs"),
    )
    out_specs = P("region", "obs", None)
    return jax.shard_map(
        functools.partial(body, mesh.shape["region"]),
        mesh=mesh, in_specs=in_specs, out_specs=out_specs, check_vma=False,
    )
```

```python
import functools

import jax
import jax.numpy as jnp
from jax import lax
from jax.experimental import pallas as pl
from jax.experimental.pallas import tpu as pltpu
from jax.sharding import PartitionSpec as P

MESH = pl.DeviceIdType.MESH
MEMBERS = 128
ROWS = MEMBERS + 16
PANEL = 16
HALF = PANEL // 2
LAG = 2
GROUP = 2
F32 = jnp.float32
BF16 = jnp.bfloat16


def iotas(shape):
    row = lax.broadcasted_iota(jnp.int32, shape, len(shape) - 2)
    col = lax.broadcasted_iota(jnp.int32, shape, len(shape) - 1)
    return row, col


def gram_kernel(
    n_region, y_hbm, d_ref, count_ref, gath, ybuf, dbuf, part, recv,
    y_sem, xs_sem, xr_sem, ups_sem, upr_sem, dns_sem, dnr_sem,
):
    pairs, _, slots, _ = ybuf.shape
    x = lax.axis_index("obs")
    me = lax.axis_index("region")
    partner = {"obs": 1 - x}
    right = {"region": lax.rem(me + 1, n_region)}
    left = {"region": lax.rem(me + n_region - 1, n_region)}

    def fetch(p):
        return pltpu.make_async_copy(y_hbm.at[pl.ds(2 * p, 2)], ybuf.at[p], y_sem.at[p])

    def swap(p):
        return pltpu.make_async_remote_copy(
            src_ref=part.at[p], dst_ref=recv.at[p], send_sem=xs_sem.at[p], recv_sem=xr_sem.at[p],
            device_id=partner, device_id_type=MESH,
        )

    def up(q):
        return pltpu.make_async_remote_copy(
            src_ref=gath.at[pairs + q], dst_ref=gath.at[q], send_sem=ups_sem.at[q],
            recv_sem=upr_sem.at[q], device_id=right, device_id_type=MESH,
        )

    def down(q):
        return pltpu.make_async_remote_copy(
            src_ref=gath.at[pairs + q], dst_ref=gath.at[2 * pairs + q], send_sem=dns_sem.at[q],
            recv_sem=dnr_sem.at[q], device_id=left, device_id_type=MESH,
        )

    def each(first, last, step):
        lax.fori_loop(first, last, lambda i, c: (step(i), c)[1], 0)

    each(0, pairs, lambda p: fetch(p).start())
    barrier = pltpu.get_barrier_semaphore()
    for other in (partner, left, right):
        pl.semaphore_signal(barrier, inc=1, device_id=other, device_id_type=MESH)
    dbuf[...] = d_ref[...].astype(F32)
    pl.semaphore_wait(barrier, 3)

    row, col = iotas((MEMBERS, MEMBERS))
    ext_row, _ = iotas((ROWS - MEMBERS, MEMBERS))
    slot_lane = lax.broadcasted_iota(jnp.int32, (1, slots), 1)

    def gram(g, y):
        live = jnp.where(slot_lane < count_ref[g] - x * slots, 1.0, 0.0).astype(BF16)
        d = jnp.broadcast_to(dbuf[pl.ds(g, 1), :], (ROWS - MEMBERS, slots)).astype(BF16)
        both = jnp.concatenate([y.T, d], axis=0) * live
        found = jnp.dot(both, y, preferred_element_type=F32)
        return found[:MEMBERS], found[MEMBERS : MEMBERS + 1]

    def grams(s):
        for i in range(GROUP):
            fetch(s * GROUP + i).wait()
        for i in range(GROUP):
            p = s * GROUP + i
            gram0, proj0 = gram(2 * p, ybuf[p, 0])
            gram1, proj1 = gram(2 * p + 1, ybuf[p, 1])
            part[p, :MEMBERS] = jnp.where(row <= col, gram0, gram1).astype(BF16)
            diag = jnp.sum(jnp.where(row == col, gram1, 0.0), axis=0, keepdims=True)
            ext = jnp.where(ext_row == 0, diag, jnp.where(ext_row == 1, proj0, jnp.where(ext_row == 2, proj1, 0.0)))
            part[p, MEMBERS:] = ext.astype(BF16)
        for i in range(GROUP):
            swap(s * GROUP + i).start()

    def forward(s):
        for i in range(GROUP):
            swap(s * GROUP + i).wait_recv()
        for i in range(GROUP):
            q = s * GROUP + i
            gath[pairs + q] = (part[q].astype(F32) + recv[q].astype(F32)).astype(BF16)
        for i in range(GROUP):
            up(s * GROUP + i).start()
            down(s * GROUP + i).start()

    groups = pairs // GROUP
    each(0, LAG, grams)

    def both(s):
        grams(s)
        forward(s - LAG)

    each(LAG, groups, both)
    each(groups - LAG, groups, forward)

    def finish(q):
        swap(q).wait_send()
        up(q).wait()
        down(q).wait()

    each(0, pairs, finish)


def solve_kernel(
    total, near_ref, taper_ref, gath, par_hbm, mean_ref, out_hbm, mat, proj, pmt, parbuf, outbuf, in_sem, out_sem
):
    regions = mat.shape[0]
    near = taper_ref.shape[0]
    before = total + regions - lax.axis_index("region") * regions

    def fetch(g):
        return pltpu.make_async_copy(par_hbm.at[g], parbuf.at[g], in_sem.at[g])

    def put(g):
        return pltpu.make_async_copy(outbuf.at[g], out_hbm.at[g], out_sem.at[g])

    def each(first, last, step, unroll=1):
        lax.fori_loop(first, last, lambda i, c: (step(i), c)[1], 0, unroll=unroll)

    each(0, regions, lambda g: fetch(g).start())

    pm = mean_ref[...]
    high = pm.astype(BF16).astype(F32)
    mid = (pm - high).astype(BF16).astype(F32)
    low = pm - high - mid
    pad = jnp.zeros((MEMBERS - 3 * regions, pm.shape[1]), F32)
    pmt[...] = jnp.concatenate([high, mid, low, pad], axis=0).T.astype(BF16)

    row, col = iotas((MEMBERS, MEMBERS))
    upper = row <= col
    diagonal = row == col

    def combine(g):
        acc = jnp.zeros((MEMBERS, MEMBERS), F32)
        ext = jnp.zeros((ROWS - MEMBERS, MEMBERS), F32)
        ext_row, _ = iotas((ROWS - MEMBERS, MEMBERS))
        for k in range(near):
            place = lax.rem(near_ref[k, g] + before, total)
            weight = taper_ref[k, g]
            odd = place % 2
            even_w = jnp.where(odd == 0, weight, 0.0)
            odd_w = jnp.where(odd == 0, 0.0, weight)
            tile = gath[place // 2].astype(F32)
            acc = acc + jnp.where(upper, even_w, odd_w) * tile[:MEMBERS]
            ext = ext + jnp.where(ext_row == 1, even_w, odd_w) * tile[MEMBERS:]
        other = jnp.where(diagonal, ext[0:1] + (MEMBERS - 1.0), acc.T)
        mat[g] = acc + other
        proj[g] = jnp.broadcast_to(ext[1:2] + ext[2:3], (8, MEMBERS))

    each(0, regions, combine, 2)

    h_row, h_lane = iotas((regions, HALF, MEMBERS))
    t_row, t_lane = iotas((HALF, MEMBERS))
    p_row, p_lane = iotas((PANEL, MEMBERS))

    def shape(a):
        return jnp.broadcast_to(a, (regions, HALF, MEMBERS))

    def eliminate(part, offset):
        for i in range(HALF):
            j = offset + i
            col_j = shape(part[:, :, j : j + 1])
            root = lax.rsqrt(shape(col_j[:, i : i + 1]))
            pivot = jnp.where(h_lane == j, 1.0, shape(part[:, i : i + 1])) * root
            factor = jnp.where(h_row > i, col_j * root, jnp.where(h_row == i, -1.0, 0.0))
            drop = (h_row == i) | ((h_lane == j) & (h_row > i))
            part = jnp.where(drop, 0.0, part) - factor * pivot
        return part

    def below(top, bot):
        for j in range(HALF):
            pivot = jnp.broadcast_to(top[j : j + 1], (HALF, MEMBERS))
            root = jnp.broadcast_to(top[j : j + 1, j : j + 1], (HALF, MEMBERS))
            factor = jnp.broadcast_to(bot[:, j : j + 1], (HALF, MEMBERS)) * root
            bot = jnp.where(t_lane == j, 0.0, bot) - factor * pivot
        return bot

    def panel(base, p):
        start = pl.multiple_of(p * PANEL, PANEL)
        slab = mat[:, pl.ds(start, PANEL), :].reshape(regions * PANEL, MEMBERS)
        slab = pltpu.roll(slab, lax.rem(MEMBERS - start, MEMBERS), 1).reshape(regions, PANEL, MEMBERS)
        top = eliminate(slab[:, :HALF], 0)
        bot = jnp.stack([below(top[g], slab[g, HALF:]) for g in range(regions)])
        bot = eliminate(bot, HALF)
        slab = jnp.concatenate([top, bot], axis=1)
        slab = pltpu.roll(slab.reshape(regions * PANEL, MEMBERS), start, 1).reshape(regions, PANEL, MEMBERS)
        mat[:, pl.ds(start, PANEL), :] = slab
        later = p_lane >= start + PANEL
        strict = (p_lane < start + PANEL) & (p_lane - start > p_row)
        clear = (row[base:] >= start + PANEL) & (col[base:] >= start) & (col[base:] < start + PANEL)
        zeros = jnp.zeros((4 * PANEL, MEMBERS), BF16)
        for g in range(0, regions, 2):
            left, right = [], []
            for h in (g, g + 1):
                full = jnp.where(strict, 0.0, slab[h])
                full_h = full.astype(BF16).astype(F32)
                full_l = full - full_h
                factor_h = jnp.where(later, full_h, 0.0)
                factor_l = jnp.where(later, full_l, 0.0)
                left += [factor_h, factor_h, factor_l, factor_l]
                right.append(jnp.concatenate([full_h, full_l, full_h, full_l], axis=0).astype(BF16))
            turned = jnp.concatenate(left, axis=0).T[base:].astype(BF16)
            blocks = jnp.concatenate(
                [
                    jnp.concatenate([right[0], zeros], axis=1),
                    jnp.concatenate([zeros, right[1]], axis=1),
                ],
                axis=0,
            )
            update = jnp.dot(turned, blocks, preferred_element_type=F32)
            mat[g, base:] = jnp.where(clear, 0.0, mat[g, base:]) - update[:, :MEMBERS]
            mat[g + 1, base:] = jnp.where(clear, 0.0, mat[g + 1, base:]) - update[:, MEMBERS:]

    steps = MEMBERS // PANEL
    parts = 4
    for part in range(parts):
        first, last = part * steps // parts, (part + 1) * steps // parts
        each(first, last, functools.partial(panel, first * PANEL))

    def apply(g):
        inverse = jnp.where(row >= col, mat[g], 0.0)
        step = jnp.sum(inverse * proj[g, 0:1, :], axis=1, keepdims=True)
        mean_weight = jnp.sum(inverse * step, axis=0, keepdims=True)
        transform = (mean_weight + (MEMBERS - 1.0) ** 0.5 * inverse).astype(BF16)
        pick = (col == g) | (col == regions + g) | (col == 2 * regions + g)
        ones = jnp.where(pick, 1.0, 0.0).astype(BF16)
        fetch(g).wait()
        moved = lax.dot_general(
            jnp.concatenate([parbuf[g], pmt[...]], axis=1),
            jnp.concatenate([transform, ones], axis=1),
            (((1,), (1,)), ((), ())),
            preferred_element_type=F32,
        )
        outbuf[g] = moved.astype(BF16)
        put(g).start()

    each(0, regions, apply, 4)
    each(0, regions, lambda g: put(g).wait())


def body(n_region, obs_anomaly, innovation, obs_count, neighbour, taper, param_anomaly, param_mean):
    regions, slots, _ = obs_anomaly.shape
    pars = param_anomaly.shape[1]
    pairs = regions // 2
    vmem = pl.BlockSpec(memory_space=pltpu.VMEM)
    smem = pl.BlockSpec(memory_space=pltpu.SMEM)
    hbm = pl.BlockSpec(memory_space=pltpu.HBM)
    gath = pl.pallas_call(
        functools.partial(gram_kernel, n_region),
        out_shape=jax.ShapeDtypeStruct((3 * pairs, ROWS, MEMBERS), BF16),
        in_specs=[hbm, vmem, smem],
        out_specs=vmem,
        scratch_shapes=[
            pltpu.VMEM((pairs, 2, slots, MEMBERS), BF16),
            pltpu.VMEM((regions, slots), F32),
            pltpu.VMEM((pairs, ROWS, MEMBERS), BF16),
            pltpu.VMEM((pairs, ROWS, MEMBERS), BF16),
        ]
        + [pltpu.SemaphoreType.DMA((pairs,))] * 7,
        compiler_params=pltpu.CompilerParams(
            collective_id=0, has_side_effects=True, vmem_limit_bytes=60 * 2**20
        ),
    )(obs_anomaly, innovation, obs_count)

    return pl.pallas_call(
        functools.partial(solve_kernel, regions * n_region),
        out_shape=jax.ShapeDtypeStruct((regions, pars, MEMBERS), BF16),
        in_specs=[smem, smem, vmem, hbm, vmem],
        out_specs=hbm,
        scratch_shapes=[
            pltpu.VMEM((regions, MEMBERS, MEMBERS), F32),
            pltpu.VMEM((regions, 8, MEMBERS), F32),
            pltpu.VMEM((pars, MEMBERS), BF16),
            pltpu.VMEM((regions, pars, MEMBERS), BF16),
            pltpu.VMEM((regions, pars, MEMBERS), BF16),
            pltpu.SemaphoreType.DMA((regions,)),
            pltpu.SemaphoreType.DMA((regions,)),
        ],
        compiler_params=pltpu.CompilerParams(vmem_limit_bytes=60 * 2**20),
    )(neighbour.T, taper.T, gath, param_anomaly, param_mean)


def solution(mesh):
    in_specs = (
        P("region", "obs", None),
        P("region", "obs"),
        P("region"),
        P("region", None),
        P("region", None),
        P("region", "obs", None),
        P("region", "obs"),
    )
    out_specs = P("region", "obs", None)
    return jax.shard_map(
        functools.partial(body, mesh.shape["region"]),
        mesh=mesh, in_specs=in_specs, out_specs=out_specs, check_vma=False,
    )
```

```python
import functools

import jax
import jax.numpy as jnp
from jax import lax
from jax.experimental import pallas as pl
from jax.experimental.pallas import tpu as pltpu
from jax.sharding import PartitionSpec as P

MESH = pl.DeviceIdType.MESH
MEMBERS = 128
ROWS = MEMBERS + 16
PANEL = 16
HALF = PANEL // 2
LAG = 2
GROUP = 2
BATCH = 4
F32 = jnp.float32
BF16 = jnp.bfloat16


def iotas(shape):
    row = lax.broadcasted_iota(jnp.int32, shape, len(shape) - 2)
    col = lax.broadcasted_iota(jnp.int32, shape, len(shape) - 1)
    return row, col


def gram_kernel(
    n_region, y_hbm, d_ref, count_ref, gath, ybuf, dbuf, part, recv,
    y_sem, xs_sem, xr_sem, ups_sem, upr_sem, dns_sem, dnr_sem,
):
    pairs, _, slots, _ = ybuf.shape
    x = lax.axis_index("obs")
    me = lax.axis_index("region")
    partner = {"obs": 1 - x}
    right = {"region": lax.rem(me + 1, n_region)}
    left = {"region": lax.rem(me + n_region - 1, n_region)}

    def fetch(p):
        return pltpu.make_async_copy(y_hbm.at[pl.ds(2 * p, 2)], ybuf.at[p], y_sem.at[p])

    def swap(p):
        return pltpu.make_async_remote_copy(
            src_ref=part.at[p], dst_ref=recv.at[p], send_sem=xs_sem.at[p], recv_sem=xr_sem.at[p],
            device_id=partner, device_id_type=MESH,
        )

    def up(q):
        return pltpu.make_async_remote_copy(
            src_ref=gath.at[pairs + q], dst_ref=gath.at[q], send_sem=ups_sem.at[q],
            recv_sem=upr_sem.at[q], device_id=right, device_id_type=MESH,
        )

    def down(q):
        return pltpu.make_async_remote_copy(
            src_ref=gath.at[pairs + q], dst_ref=gath.at[2 * pairs + q], send_sem=dns_sem.at[q],
            recv_sem=dnr_sem.at[q], device_id=left, device_id_type=MESH,
        )

    def each(first, last, step):
        lax.fori_loop(first, last, lambda i, c: (step(i), c)[1], 0)

    each(0, pairs, lambda p: fetch(p).start())
    barrier = pltpu.get_barrier_semaphore()
    for other in (partner, left, right):
        pl.semaphore_signal(barrier, inc=1, device_id=other, device_id_type=MESH)
    dbuf[...] = d_ref[...].astype(F32)
    pl.semaphore_wait(barrier, 3)

    row, col = iotas((MEMBERS, MEMBERS))
    ext_row, _ = iotas((ROWS - MEMBERS, MEMBERS))
    slot_lane = lax.broadcasted_iota(jnp.int32, (1, slots), 1)

    def gram(g, y):
        live = jnp.where(slot_lane < count_ref[g] - x * slots, 1.0, 0.0).astype(BF16)
        d = jnp.broadcast_to(dbuf[pl.ds(g, 1), :], (ROWS - MEMBERS, slots)).astype(BF16)
        both = jnp.concatenate([y.T, d], axis=0) * live
        found = jnp.dot(both, y, preferred_element_type=F32)
        return found[:MEMBERS], found[MEMBERS : MEMBERS + 1]

    def grams(s):
        for i in range(GROUP):
            fetch(s * GROUP + i).wait()
        for i in range(GROUP):
            p = s * GROUP + i
            gram0, proj0 = gram(2 * p, ybuf[p, 0])
            gram1, proj1 = gram(2 * p + 1, ybuf[p, 1])
            part[p, :MEMBERS] = jnp.where(row <= col, gram0, gram1).astype(BF16)
            diag = jnp.sum(jnp.where(row == col, gram1, 0.0), axis=0, keepdims=True)
            ext = jnp.where(ext_row == 0, diag, jnp.where(ext_row == 1, proj0, jnp.where(ext_row == 2, proj1, 0.0)))
            part[p, MEMBERS:] = ext.astype(BF16)
        for i in range(GROUP):
            swap(s * GROUP + i).start()

    def forward(s):
        for i in range(GROUP):
            swap(s * GROUP + i).wait_recv()
        for i in range(GROUP):
            q = s * GROUP + i
            gath[pairs + q] = (part[q].astype(F32) + recv[q].astype(F32)).astype(BF16)
        for i in range(GROUP):
            up(s * GROUP + i).start()
            down(s * GROUP + i).start()

    groups = pairs // GROUP
    each(0, LAG, grams)

    def both(s):
        grams(s)
        forward(s - LAG)

    each(LAG, groups, both)
    each(groups - LAG, groups, forward)

    def finish(q):
        swap(q).wait_send()
        up(q).wait()
        down(q).wait()

    each(0, pairs, finish)


def solve_kernel(
    total, near_ref, taper_ref, gath, par_hbm, mean_ref, out_hbm, mat, proj, pmt, parbuf, outbuf, in_sem, out_sem
):
    regions = mat.shape[0]
    near = taper_ref.shape[0]
    before = total + regions - lax.axis_index("region") * regions

    def fetch(g):
        return pltpu.make_async_copy(par_hbm.at[g], parbuf.at[g], in_sem.at[g])

    def put(g):
        return pltpu.make_async_copy(outbuf.at[g], out_hbm.at[g], out_sem.at[g])

    def each(first, last, step, unroll=1):
        lax.fori_loop(first, last, lambda i, c: (step(i), c)[1], 0, unroll=unroll)

    each(0, regions, lambda g: fetch(g).start())

    pm = mean_ref[...]
    high = pm.astype(BF16).astype(F32)
    mid = (pm - high).astype(BF16).astype(F32)
    low = pm - high - mid
    pad = jnp.zeros((MEMBERS - 3 * regions, pm.shape[1]), F32)
    pmt[...] = jnp.concatenate([high, mid, low, pad], axis=0).T.astype(BF16)

    row, col = iotas((MEMBERS, MEMBERS))
    upper = row <= col
    diagonal = row == col

    ext_row, _ = iotas((ROWS - MEMBERS, MEMBERS))

    def combined(g):
        acc, ext = 0.0, 0.0
        for k in range(near):
            place = lax.rem(near_ref[k, g] + before, total)
            weight = taper_ref[k, g]
            odd = lax.bitwise_and(place, 1)
            odd_w = weight * odd.astype(F32)
            even_w = weight - odd_w
            tile = gath[lax.shift_right_logical(place, 1)].astype(F32)
            acc = acc + jnp.where(upper, even_w, odd_w) * tile[:MEMBERS]
            ext = ext + jnp.where(ext_row == 1, even_w, odd_w) * tile[MEMBERS:]
        other = jnp.where(diagonal, ext[0:1] + (MEMBERS - 1.0), acc.T)
        return acc + other, jnp.broadcast_to(ext[1:2] + ext[2:3], (8, MEMBERS))

    def combine(s):
        for i, (matrix, vector) in enumerate([combined(s * BATCH + i) for i in range(BATCH)]):
            mat[s * BATCH + i] = matrix
            proj[s * BATCH + i] = vector

    each(0, regions // BATCH, combine)

    h_row, h_lane = iotas((regions, HALF, MEMBERS))
    t_row, t_lane = iotas((HALF, MEMBERS))
    p_row, p_lane = iotas((PANEL, MEMBERS))

    def shape(a):
        return jnp.broadcast_to(a, (regions, HALF, MEMBERS))

    def eliminate(part, offset):
        for i in range(HALF):
            j = offset + i
            col_j = shape(part[:, :, j : j + 1])
            root = lax.rsqrt(shape(col_j[:, i : i + 1]))
            pivot = jnp.where(h_lane == j, 1.0, shape(part[:, i : i + 1])) * root
            factor = jnp.where(h_row > i, col_j * root, jnp.where(h_row == i, -1.0, 0.0))
            drop = (h_row == i) | ((h_lane == j) & (h_row > i))
            part = jnp.where(drop, 0.0, part) - factor * pivot
        return part

    def below(top, bot):
        for j in range(HALF):
            pivot = jnp.broadcast_to(top[j : j + 1], (HALF, MEMBERS))
            root = jnp.broadcast_to(top[j : j + 1, j : j + 1], (HALF, MEMBERS))
            factor = jnp.broadcast_to(bot[:, j : j + 1], (HALF, MEMBERS)) * root
            bot = jnp.where(t_lane == j, 0.0, bot) - factor * pivot
        return bot

    def panel(base, p):
        start = pl.multiple_of(p * PANEL, PANEL)
        slab = mat[:, pl.ds(start, PANEL), :].reshape(regions * PANEL, MEMBERS)
        slab = pltpu.roll(slab, lax.rem(MEMBERS - start, MEMBERS), 1).reshape(regions, PANEL, MEMBERS)
        top = eliminate(slab[:, :HALF], 0)
        bot = jnp.stack([below(top[g], slab[g, HALF:]) for g in range(regions)])
        bot = eliminate(bot, HALF)
        slab = jnp.concatenate([top, bot], axis=1)
        slab = pltpu.roll(slab.reshape(regions * PANEL, MEMBERS), start, 1).reshape(regions, PANEL, MEMBERS)
        mat[:, pl.ds(start, PANEL), :] = slab
        later = p_lane >= start + PANEL
        strict = (p_lane < start + PANEL) & (p_lane - start > p_row)
        clear = (row[base:] >= start + PANEL) & (col[base:] >= start) & (col[base:] < start + PANEL)
        zeros = jnp.zeros((4 * PANEL, MEMBERS), BF16)
        for g in range(0, regions, 2):
            left, right = [], []
            for h in (g, g + 1):
                full = jnp.where(strict, 0.0, slab[h])
                full_h = full.astype(BF16).astype(F32)
                full_l = full - full_h
                factor_h = jnp.where(later, full_h, 0.0)
                factor_l = jnp.where(later, full_l, 0.0)
                left += [factor_h, factor_h, factor_l, factor_l]
                right.append(jnp.concatenate([full_h, full_l, full_h, full_l], axis=0).astype(BF16))
            turned = jnp.concatenate(left, axis=0).T[base:].astype(BF16)
            blocks = jnp.concatenate(
                [
                    jnp.concatenate([right[0], zeros], axis=1),
                    jnp.concatenate([zeros, right[1]], axis=1),
                ],
                axis=0,
            )
            update = jnp.dot(turned, blocks, preferred_element_type=F32)
            mat[g, base:] = jnp.where(clear, 0.0, mat[g, base:]) - update[:, :MEMBERS]
            mat[g + 1, base:] = jnp.where(clear, 0.0, mat[g + 1, base:]) - update[:, MEMBERS:]

    steps = MEMBERS // PANEL
    parts = 4
    for part in range(parts):
        first, last = part * steps // parts, (part + 1) * steps // parts
        each(first, last, functools.partial(panel, first * PANEL))

    means = pmt[...]

    def update_of(g):
        inverse = jnp.where(row >= col, mat[g], 0.0)
        step = jnp.sum(inverse * proj[g, 0:1, :], axis=1, keepdims=True)
        mean_weight = jnp.sum(inverse * step, axis=0, keepdims=True)
        transform = (mean_weight + (MEMBERS - 1.0) ** 0.5 * inverse).astype(BF16)
        pick = (col == g) | (col == regions + g) | (col == 2 * regions + g)
        ones = jnp.where(pick, 1.0, 0.0).astype(BF16)
        return jnp.concatenate([transform, ones], axis=1)

    def apply(s):
        for i in range(BATCH):
            fetch(s * BATCH + i).wait()
        weights = [update_of(s * BATCH + i) for i in range(BATCH)]
        for i in range(BATCH):
            moved = lax.dot_general(
                jnp.concatenate([parbuf[s * BATCH + i], means], axis=1),
                weights[i],
                (((1,), (1,)), ((), ())),
                preferred_element_type=F32,
            )
            outbuf[s * BATCH + i] = moved.astype(BF16)
        for i in range(BATCH):
            put(s * BATCH + i).start()

    each(0, regions // BATCH, apply)
    each(0, regions, lambda g: put(g).wait())


def body(n_region, obs_anomaly, innovation, obs_count, neighbour, taper, param_anomaly, param_mean):
    regions, slots, _ = obs_anomaly.shape
    pars = param_anomaly.shape[1]
    pairs = regions // 2
    vmem = pl.BlockSpec(memory_space=pltpu.VMEM)
    smem = pl.BlockSpec(memory_space=pltpu.SMEM)
    hbm = pl.BlockSpec(memory_space=pltpu.HBM)
    gath = pl.pallas_call(
        functools.partial(gram_kernel, n_region),
        out_shape=jax.ShapeDtypeStruct((3 * pairs, ROWS, MEMBERS), BF16),
        in_specs=[hbm, vmem, smem],
        out_specs=vmem,
        scratch_shapes=[
            pltpu.VMEM((pairs, 2, slots, MEMBERS), BF16),
            pltpu.VMEM((regions, slots), F32),
            pltpu.VMEM((pairs, ROWS, MEMBERS), BF16),
            pltpu.VMEM((pairs, ROWS, MEMBERS), BF16),
        ]
        + [pltpu.SemaphoreType.DMA((pairs,))] * 7,
        compiler_params=pltpu.CompilerParams(
            collective_id=0, has_side_effects=True, vmem_limit_bytes=60 * 2**20
        ),
    )(obs_anomaly, innovation, obs_count)

    return pl.pallas_call(
        functools.partial(solve_kernel, regions * n_region),
        out_shape=jax.ShapeDtypeStruct((regions, pars, MEMBERS), BF16),
        in_specs=[smem, smem, vmem, hbm, vmem],
        out_specs=hbm,
        scratch_shapes=[
            pltpu.VMEM((regions, MEMBERS, MEMBERS), F32),
            pltpu.VMEM((regions, 8, MEMBERS), F32),
            pltpu.VMEM((pars, MEMBERS), BF16),
            pltpu.VMEM((regions, pars, MEMBERS), BF16),
            pltpu.VMEM((regions, pars, MEMBERS), BF16),
            pltpu.SemaphoreType.DMA((regions,)),
            pltpu.SemaphoreType.DMA((regions,)),
        ],
        compiler_params=pltpu.CompilerParams(vmem_limit_bytes=60 * 2**20),
    )(neighbour.T, taper.T, gath, param_anomaly, param_mean)


def solution(mesh):
    in_specs = (
        P("region", "obs", None),
        P("region", "obs"),
        P("region"),
        P("region", None),
        P("region", None),
        P("region", "obs", None),
        P("region", "obs"),
    )
    out_specs = P("region", "obs", None)
    return jax.shard_map(
        functools.partial(body, mesh.shape["region"]),
        mesh=mesh, in_specs=in_specs, out_specs=out_specs, check_vma=False,
    )
```

```python
import functools

import jax
import jax.numpy as jnp
from jax import lax
from jax.experimental import pallas as pl
from jax.experimental.pallas import tpu as pltpu
from jax.sharding import PartitionSpec as P

MESH = pl.DeviceIdType.MESH
MEMBERS = 128
ROWS = MEMBERS + 16
PANEL = 16
HALF = PANEL // 2
LAG = 1
GROUP = 2
BATCH = 8
F32 = jnp.float32
BF16 = jnp.bfloat16


def iotas(shape):
    row = lax.broadcasted_iota(jnp.int32, shape, len(shape) - 2)
    col = lax.broadcasted_iota(jnp.int32, shape, len(shape) - 1)
    return row, col


def gram_kernel(
    n_region, y_hbm, d_ref, count_ref, gath, ybuf, dbuf, part, recv,
    y_sem, xs_sem, xr_sem, ups_sem, upr_sem, dns_sem, dnr_sem,
):
    pairs, _, slots, _ = ybuf.shape
    x = lax.axis_index("obs")
    me = lax.axis_index("region")
    partner = {"obs": 1 - x}
    right = {"region": lax.rem(me + 1, n_region)}
    left = {"region": lax.rem(me + n_region - 1, n_region)}

    def fetch(p):
        return pltpu.make_async_copy(y_hbm.at[pl.ds(2 * p, 2)], ybuf.at[p], y_sem.at[p])

    def swap(p):
        return pltpu.make_async_remote_copy(
            src_ref=part.at[p], dst_ref=recv.at[p], send_sem=xs_sem.at[p], recv_sem=xr_sem.at[p],
            device_id=partner, device_id_type=MESH,
        )

    def up(q):
        return pltpu.make_async_remote_copy(
            src_ref=gath.at[pairs + q], dst_ref=gath.at[q], send_sem=ups_sem.at[q],
            recv_sem=upr_sem.at[q], device_id=right, device_id_type=MESH,
        )

    def down(q):
        return pltpu.make_async_remote_copy(
            src_ref=gath.at[pairs + q], dst_ref=gath.at[2 * pairs + q], send_sem=dns_sem.at[q],
            recv_sem=dnr_sem.at[q], device_id=left, device_id_type=MESH,
        )

    def each(first, last, step):
        lax.fori_loop(first, last, lambda i, c: (step(i), c)[1], 0)

    each(0, pairs, lambda p: fetch(p).start())
    barrier = pltpu.get_barrier_semaphore()
    for other in (partner, left, right):
        pl.semaphore_signal(barrier, inc=1, device_id=other, device_id_type=MESH)
    dbuf[...] = d_ref[...].astype(F32)
    pl.semaphore_wait(barrier, 3)

    row, col = iotas((MEMBERS, MEMBERS))
    ext_row, _ = iotas((ROWS - MEMBERS, MEMBERS))
    slot_lane = lax.broadcasted_iota(jnp.int32, (1, slots), 1)

    def gram(g, y):
        live = jnp.where(slot_lane < count_ref[g] - x * slots, 1.0, 0.0).astype(BF16)
        d = jnp.broadcast_to(dbuf[pl.ds(g, 1), :], (ROWS - MEMBERS, slots)).astype(BF16)
        both = jnp.concatenate([y.T, d], axis=0) * live
        found = jnp.dot(both, y, preferred_element_type=F32)
        return found[:MEMBERS], found[MEMBERS : MEMBERS + 1]

    def grams(s):
        for i in range(GROUP):
            fetch(s * GROUP + i).wait()
        for i in range(GROUP):
            p = s * GROUP + i
            gram0, proj0 = gram(2 * p, ybuf[p, 0])
            gram1, proj1 = gram(2 * p + 1, ybuf[p, 1])
            part[p, :MEMBERS] = jnp.where(row <= col, gram0, gram1).astype(BF16)
            diag = jnp.sum(jnp.where(row == col, gram1, 0.0), axis=0, keepdims=True)
            ext = jnp.where(ext_row == 0, diag, jnp.where(ext_row == 1, proj0, jnp.where(ext_row == 2, proj1, 0.0)))
            part[p, MEMBERS:] = ext.astype(BF16)
        for i in range(GROUP):
            swap(s * GROUP + i).start()

    def forward(s):
        for i in range(GROUP):
            swap(s * GROUP + i).wait_recv()
        for i in range(GROUP):
            q = s * GROUP + i
            gath[pairs + q] = (part[q].astype(F32) + recv[q].astype(F32)).astype(BF16)
        for i in range(GROUP):
            up(s * GROUP + i).start()
            down(s * GROUP + i).start()

    groups = pairs // GROUP
    each(0, LAG, grams)

    def both(s):
        grams(s)
        forward(s - LAG)

    each(LAG, groups, both)
    each(groups - LAG, groups, forward)

    def finish(q):
        swap(q).wait_send()
        up(q).wait()
        down(q).wait()

    each(0, pairs, finish)


def solve_kernel(
    total, near_ref, taper_ref, gath, par_hbm, mean_ref, out_hbm, mat, proj, pmt, parbuf, outbuf, in_sem, out_sem
):
    regions = mat.shape[0]
    near = taper_ref.shape[0]
    before = total + regions - lax.axis_index("region") * regions

    def fetch(g):
        return pltpu.make_async_copy(par_hbm.at[g], parbuf.at[g], in_sem.at[g])

    def put(g):
        return pltpu.make_async_copy(outbuf.at[g], out_hbm.at[g], out_sem.at[g])

    def each(first, last, step, unroll=1):
        lax.fori_loop(first, last, lambda i, c: (step(i), c)[1], 0, unroll=unroll)

    each(0, regions, lambda g: fetch(g).start())

    pm = mean_ref[...]
    high = pm.astype(BF16).astype(F32)
    mid = (pm - high).astype(BF16).astype(F32)
    low = pm - high - mid
    pad = jnp.zeros((MEMBERS - 3 * regions, pm.shape[1]), F32)
    pmt[...] = jnp.concatenate([high, mid, low, pad], axis=0).T.astype(BF16)

    row, col = iotas((MEMBERS, MEMBERS))
    upper = row <= col
    diagonal = row == col

    ext_row, _ = iotas((ROWS - MEMBERS, MEMBERS))

    def combined(g):
        acc, ext = 0.0, 0.0
        for k in range(near):
            place = lax.rem(near_ref[k, g] + before, total)
            weight = taper_ref[k, g]
            odd = lax.bitwise_and(place, 1)
            odd_w = weight * odd.astype(F32)
            even_w = weight - odd_w
            tile = gath[lax.shift_right_logical(place, 1)].astype(F32)
            acc = acc + jnp.where(upper, even_w, odd_w) * tile[:MEMBERS]
            ext = ext + jnp.where(ext_row == 1, even_w, odd_w) * tile[MEMBERS:]
        other = jnp.where(diagonal, ext[0:1] + (MEMBERS - 1.0), acc.T)
        return acc + other, jnp.broadcast_to(ext[1:2] + ext[2:3], (8, MEMBERS))

    def combine(s):
        for i, (matrix, vector) in enumerate([combined(s * BATCH + i) for i in range(BATCH)]):
            mat[s * BATCH + i] = matrix
            proj[s * BATCH + i] = vector

    each(0, regions // BATCH, combine)

    h_row, h_lane = iotas((regions, HALF, MEMBERS))
    t_row, t_lane = iotas((HALF, MEMBERS))
    p_row, p_lane = iotas((PANEL, MEMBERS))

    def shape(a):
        return jnp.broadcast_to(a, (regions, HALF, MEMBERS))

    def eliminate(part, offset):
        for i in range(0, HALF, 2):
            j = offset + i
            col_0, col_1 = shape(part[:, :, j : j + 1]), shape(part[:, :, j + 1 : j + 2])
            row_0, row_1 = shape(part[:, i : i + 1]), shape(part[:, i + 1 : i + 2])
            root_0 = lax.rsqrt(shape(col_0[:, i : i + 1]))
            factor_0 = col_0 * root_0
            link = shape(factor_0[:, i + 1 : i + 2])
            col_1 = col_1 - factor_0 * link
            root_1 = lax.rsqrt(shape(col_1[:, i + 1 : i + 2]))
            pivot_0 = jnp.where(h_lane == j, 1.0, row_0) * root_0
            row_1 = jnp.where(h_lane == j, 0.0, row_1) - link * pivot_0
            pivot_1 = jnp.where(h_lane == j + 1, 1.0, row_1) * root_1
            factor_0 = jnp.where(h_row > i + 1, factor_0, jnp.where(h_row == i, -1.0, 0.0))
            factor_1 = jnp.where(h_row > i + 1, col_1 * root_1, jnp.where(h_row == i + 1, -1.0, 0.0))
            drop_0 = (h_row == i) | ((h_lane == j) & (h_row > i + 1))
            drop_1 = (h_row == i + 1) | ((h_lane == j + 1) & (h_row > i + 1))
            part = jnp.where(drop_0, 0.0, part) - factor_0 * pivot_0
            part = jnp.where(drop_1, 0.0, part) - factor_1 * pivot_1
        return part

    def below(top, bot):
        for j in range(HALF):
            pivot = jnp.broadcast_to(top[j : j + 1], (HALF, MEMBERS))
            root = jnp.broadcast_to(top[j : j + 1, j : j + 1], (HALF, MEMBERS))
            factor = jnp.broadcast_to(bot[:, j : j + 1], (HALF, MEMBERS)) * root
            bot = jnp.where(t_lane == j, 0.0, bot) - factor * pivot
        return bot

    def panel(base, p):
        start = pl.multiple_of(p * PANEL, PANEL)
        slab = mat[:, pl.ds(start, PANEL), :].reshape(regions * PANEL, MEMBERS)
        slab = pltpu.roll(slab, lax.rem(MEMBERS - start, MEMBERS), 1).reshape(regions, PANEL, MEMBERS)
        top = eliminate(slab[:, :HALF], 0)
        bot = jnp.stack([below(top[g], slab[g, HALF:]) for g in range(regions)])
        bot = eliminate(bot, HALF)
        slab = jnp.concatenate([top, bot], axis=1)
        slab = pltpu.roll(slab.reshape(regions * PANEL, MEMBERS), start, 1).reshape(regions, PANEL, MEMBERS)
        mat[:, pl.ds(start, PANEL), :] = slab
        later = p_lane >= start + PANEL
        strict = (p_lane < start + PANEL) & (p_lane - start > p_row)
        clear = (row[base:] >= start + PANEL) & (col[base:] >= start) & (col[base:] < start + PANEL)
        zeros = jnp.zeros((4 * PANEL, MEMBERS), BF16)
        for g in range(0, regions, 2):
            left, right = [], []
            for h in (g, g + 1):
                full = jnp.where(strict, 0.0, slab[h])
                full_h = full.astype(BF16).astype(F32)
                full_l = full - full_h
                factor_h = jnp.where(later, full_h, 0.0)
                factor_l = jnp.where(later, full_l, 0.0)
                left += [factor_h, factor_h, factor_l, factor_l]
                right.append(jnp.concatenate([full_h, full_l, full_h, full_l], axis=0).astype(BF16))
            turned = jnp.concatenate(left, axis=0).T[base:].astype(BF16)
            blocks = jnp.concatenate(
                [
                    jnp.concatenate([right[0], zeros], axis=1),
                    jnp.concatenate([zeros, right[1]], axis=1),
                ],
                axis=0,
            )
            update = jnp.dot(turned, blocks, preferred_element_type=F32)
            mat[g, base:] = jnp.where(clear, 0.0, mat[g, base:]) - update[:, :MEMBERS]
            mat[g + 1, base:] = jnp.where(clear, 0.0, mat[g + 1, base:]) - update[:, MEMBERS:]

    steps = MEMBERS // PANEL
    parts = 4
    for part in range(parts):
        first, last = part * steps // parts, (part + 1) * steps // parts
        each(first, last, functools.partial(panel, first * PANEL))

    means = pmt[...]

    def update_of(g):
        inverse = jnp.where(row >= col, mat[g], 0.0)
        step = jnp.sum(inverse * proj[g, 0:1, :], axis=1, keepdims=True)
        mean_weight = jnp.sum(inverse * step, axis=0, keepdims=True)
        transform = (mean_weight + (MEMBERS - 1.0) ** 0.5 * inverse).astype(BF16)
        pick = (col == g) | (col == regions + g) | (col == 2 * regions + g)
        ones = jnp.where(pick, 1.0, 0.0).astype(BF16)
        return jnp.concatenate([transform, ones], axis=1)

    def apply(s):
        for i in range(BATCH):
            fetch(s * BATCH + i).wait()
        weights = [update_of(s * BATCH + i) for i in range(BATCH)]
        for i in range(BATCH):
            moved = lax.dot_general(
                jnp.concatenate([parbuf[s * BATCH + i], means], axis=1),
                weights[i],
                (((1,), (1,)), ((), ())),
                preferred_element_type=F32,
            )
            outbuf[s * BATCH + i] = moved.astype(BF16)
        for i in range(BATCH):
            put(s * BATCH + i).start()

    each(0, regions // BATCH, apply)
    each(0, regions, lambda g: put(g).wait())


def body(n_region, obs_anomaly, innovation, obs_count, neighbour, taper, param_anomaly, param_mean):
    regions, slots, _ = obs_anomaly.shape
    pars = param_anomaly.shape[1]
    pairs = regions // 2
    vmem = pl.BlockSpec(memory_space=pltpu.VMEM)
    smem = pl.BlockSpec(memory_space=pltpu.SMEM)
    hbm = pl.BlockSpec(memory_space=pltpu.HBM)
    gath = pl.pallas_call(
        functools.partial(gram_kernel, n_region),
        out_shape=jax.ShapeDtypeStruct((3 * pairs, ROWS, MEMBERS), BF16),
        in_specs=[hbm, vmem, smem],
        out_specs=vmem,
        scratch_shapes=[
            pltpu.VMEM((pairs, 2, slots, MEMBERS), BF16),
            pltpu.VMEM((regions, slots), F32),
            pltpu.VMEM((pairs, ROWS, MEMBERS), BF16),
            pltpu.VMEM((pairs, ROWS, MEMBERS), BF16),
        ]
        + [pltpu.SemaphoreType.DMA((pairs,))] * 7,
        compiler_params=pltpu.CompilerParams(
            collective_id=0, has_side_effects=True, vmem_limit_bytes=60 * 2**20
        ),
    )(obs_anomaly, innovation, obs_count)

    return pl.pallas_call(
        functools.partial(solve_kernel, regions * n_region),
        out_shape=jax.ShapeDtypeStruct((regions, pars, MEMBERS), BF16),
        in_specs=[smem, smem, vmem, hbm, vmem],
        out_specs=hbm,
        scratch_shapes=[
            pltpu.VMEM((regions, MEMBERS, MEMBERS), F32),
            pltpu.VMEM((regions, 8, MEMBERS), F32),
            pltpu.VMEM((pars, MEMBERS), BF16),
            pltpu.VMEM((regions, pars, MEMBERS), BF16),
            pltpu.VMEM((regions, pars, MEMBERS), BF16),
            pltpu.SemaphoreType.DMA((regions,)),
            pltpu.SemaphoreType.DMA((regions,)),
        ],
        compiler_params=pltpu.CompilerParams(vmem_limit_bytes=60 * 2**20),
    )(neighbour.T, taper.T, gath, param_anomaly, param_mean)


def solution(mesh):
    in_specs = (
        P("region", "obs", None),
        P("region", "obs"),
        P("region"),
        P("region", None),
        P("region", None),
        P("region", "obs", None),
        P("region", "obs"),
    )
    out_specs = P("region", "obs", None)
    return jax.shard_map(
        functools.partial(body, mesh.shape["region"]),
        mesh=mesh, in_specs=in_specs, out_specs=out_specs, check_vma=False,
    )
```

```python
import functools

import jax
import jax.numpy as jnp
from jax import lax
from jax.experimental import pallas as pl
from jax.experimental.pallas import tpu as pltpu
from jax.sharding import PartitionSpec as P

MESH = pl.DeviceIdType.MESH
MEMBERS = 128
ROWS = MEMBERS + 16
PANEL = 16
HALF = PANEL // 2
LAG = 2
GROUP = 2
BATCH = 8
F32 = jnp.float32
BF16 = jnp.bfloat16


def iotas(shape):
    row = lax.broadcasted_iota(jnp.int32, shape, len(shape) - 2)
    col = lax.broadcasted_iota(jnp.int32, shape, len(shape) - 1)
    return row, col


def gram_kernel(
    n_region, y_hbm, d_ref, count_ref, gath, ybuf, dbuf, part, recv,
    y_sem, xs_sem, xr_sem, ups_sem, upr_sem, dns_sem, dnr_sem,
):
    pairs, _, slots, _ = ybuf.shape
    x = lax.axis_index("obs")
    me = lax.axis_index("region")
    partner = {"obs": 1 - x}
    right = {"region": lax.rem(me + 1, n_region)}
    left = {"region": lax.rem(me + n_region - 1, n_region)}

    def fetch(p):
        return pltpu.make_async_copy(y_hbm.at[pl.ds(2 * p, 2)], ybuf.at[p], y_sem.at[p])

    def swap(p):
        return pltpu.make_async_remote_copy(
            src_ref=part.at[p], dst_ref=recv.at[p], send_sem=xs_sem.at[p], recv_sem=xr_sem.at[p],
            device_id=partner, device_id_type=MESH,
        )

    def up(q):
        return pltpu.make_async_remote_copy(
            src_ref=gath.at[pairs + q], dst_ref=gath.at[q], send_sem=ups_sem.at[q],
            recv_sem=upr_sem.at[q], device_id=right, device_id_type=MESH,
        )

    def down(q):
        return pltpu.make_async_remote_copy(
            src_ref=gath.at[pairs + q], dst_ref=gath.at[2 * pairs + q], send_sem=dns_sem.at[q],
            recv_sem=dnr_sem.at[q], device_id=left, device_id_type=MESH,
        )

    def each(first, last, step):
        lax.fori_loop(first, last, lambda i, c: (step(i), c)[1], 0)

    each(0, pairs, lambda p: fetch(p).start())
    barrier = pltpu.get_barrier_semaphore()
    for other in (partner, left, right):
        pl.semaphore_signal(barrier, inc=1, device_id=other, device_id_type=MESH)
    dbuf[...] = d_ref[...].astype(F32)
    pl.semaphore_wait(barrier, 3)

    row, col = iotas((MEMBERS, MEMBERS))
    ext_row, _ = iotas((ROWS - MEMBERS, MEMBERS))
    slot_lane = lax.broadcasted_iota(jnp.int32, (1, slots), 1)

    def gram(g, y):
        live = jnp.where(slot_lane < count_ref[g] - x * slots, 1.0, 0.0).astype(BF16)
        d = jnp.broadcast_to(dbuf[pl.ds(g, 1), :], (ROWS - MEMBERS, slots)).astype(BF16)
        both = jnp.concatenate([y.T, d], axis=0) * live
        found = jnp.dot(both, y, preferred_element_type=F32)
        return found[:MEMBERS], found[MEMBERS : MEMBERS + 1]

    def grams(s):
        for i in range(GROUP):
            fetch(s * GROUP + i).wait()
        for i in range(GROUP):
            p = s * GROUP + i
            gram0, proj0 = gram(2 * p, ybuf[p, 0])
            gram1, proj1 = gram(2 * p + 1, ybuf[p, 1])
            part[p, :MEMBERS] = jnp.where(row <= col, gram0, gram1).astype(BF16)
            diag = jnp.sum(jnp.where(row == col, gram1, 0.0), axis=0, keepdims=True)
            ext = jnp.where(ext_row == 0, diag, jnp.where(ext_row == 1, proj0, jnp.where(ext_row == 2, proj1, 0.0)))
            part[p, MEMBERS:] = ext.astype(BF16)
        for i in range(GROUP):
            swap(s * GROUP + i).start()

    def forward(s):
        for i in range(GROUP):
            swap(s * GROUP + i).wait_recv()
        for i in range(GROUP):
            q = s * GROUP + i
            gath[pairs + q] = (part[q].astype(F32) + recv[q].astype(F32)).astype(BF16)
        for i in range(GROUP):
            up(s * GROUP + i).start()
            down(s * GROUP + i).start()

    groups = pairs // GROUP
    each(0, LAG, grams)

    def both(s):
        grams(s)
        forward(s - LAG)

    each(LAG, groups, both)
    each(groups - LAG, groups, forward)

    def finish(q):
        swap(q).wait_send()
        up(q).wait()
        down(q).wait()

    each(0, pairs, finish)


def solve_kernel(
    total, near_ref, taper_ref, gath, par_hbm, mean_ref, out_hbm, mat, proj, pmt, parbuf, outbuf, in_sem, out_sem
):
    regions = mat.shape[0]
    near = taper_ref.shape[0]
    before = total + regions - lax.axis_index("region") * regions

    def fetch(g):
        return pltpu.make_async_copy(par_hbm.at[g], parbuf.at[g], in_sem.at[g])

    def put(g):
        return pltpu.make_async_copy(outbuf.at[g], out_hbm.at[g], out_sem.at[g])

    def each(first, last, step, unroll=1):
        lax.fori_loop(first, last, lambda i, c: (step(i), c)[1], 0, unroll=unroll)

    each(0, regions, lambda g: fetch(g).start())

    pm = mean_ref[...]
    high = pm.astype(BF16).astype(F32)
    mid = (pm - high).astype(BF16).astype(F32)
    low = pm - high - mid
    pad = jnp.zeros((MEMBERS - 3 * regions, pm.shape[1]), F32)
    pmt[...] = jnp.concatenate([high, mid, low, pad], axis=0).T.astype(BF16)

    row, col = iotas((MEMBERS, MEMBERS))
    upper = row <= col
    diagonal = row == col

    ext_row, _ = iotas((ROWS - MEMBERS, MEMBERS))

    def combined(g):
        acc, ext = 0.0, 0.0
        for k in range(near):
            place = lax.rem(near_ref[k, g] + before, total)
            weight = taper_ref[k, g]
            odd = lax.bitwise_and(place, 1)
            odd_w = weight * odd.astype(F32)
            even_w = weight - odd_w
            tile = gath[lax.shift_right_logical(place, 1)].astype(F32)
            acc = acc + jnp.where(upper, even_w, odd_w) * tile[:MEMBERS]
            ext = ext + jnp.where(ext_row == 1, even_w, odd_w) * tile[MEMBERS:]
        other = jnp.where(diagonal, ext[0:1] + (MEMBERS - 1.0), acc.T)
        return acc + other, jnp.broadcast_to(ext[1:2] + ext[2:3], (8, MEMBERS))

    def combine(s):
        for i, (matrix, vector) in enumerate([combined(s * BATCH + i) for i in range(BATCH)]):
            mat[s * BATCH + i] = matrix
            proj[s * BATCH + i] = vector

    each(0, regions // BATCH, combine)

    h_row, h_lane = iotas((regions, HALF, MEMBERS))
    t_row, t_lane = iotas((HALF, MEMBERS))
    p_row, p_lane = iotas((PANEL, MEMBERS))

    def shape(a):
        return jnp.broadcast_to(a, (regions, HALF, MEMBERS))

    def eliminate(part, offset):
        for i in range(0, HALF, 2):
            j = offset + i
            col_0, col_1 = shape(part[:, :, j : j + 1]), shape(part[:, :, j + 1 : j + 2])
            row_0, row_1 = shape(part[:, i : i + 1]), shape(part[:, i + 1 : i + 2])
            root_0 = lax.rsqrt(shape(col_0[:, i : i + 1]))
            factor_0 = col_0 * root_0
            link = shape(factor_0[:, i + 1 : i + 2])
            col_1 = col_1 - factor_0 * link
            root_1 = lax.rsqrt(shape(col_1[:, i + 1 : i + 2]))
            pivot_0 = jnp.where(h_lane == j, 1.0, row_0) * root_0
            row_1 = jnp.where(h_lane == j, 0.0, row_1) - link * pivot_0
            pivot_1 = jnp.where(h_lane == j + 1, 1.0, row_1) * root_1
            factor_0 = jnp.where(h_row > i + 1, factor_0, jnp.where(h_row == i, -1.0, 0.0))
            factor_1 = jnp.where(h_row > i + 1, col_1 * root_1, jnp.where(h_row == i + 1, -1.0, 0.0))
            drop_0 = (h_row == i) | ((h_lane == j) & (h_row > i + 1))
            drop_1 = (h_row == i + 1) | ((h_lane == j + 1) & (h_row > i + 1))
            part = jnp.where(drop_0, 0.0, part) - factor_0 * pivot_0
            part = jnp.where(drop_1, 0.0, part) - factor_1 * pivot_1
        return part

    def below(top, bot):
        for j in range(HALF):
            pivot = jnp.broadcast_to(top[j : j + 1], (HALF, MEMBERS))
            root = jnp.broadcast_to(top[j : j + 1, j : j + 1], (HALF, MEMBERS))
            factor = jnp.broadcast_to(bot[:, j : j + 1], (HALF, MEMBERS)) * root
            bot = jnp.where(t_lane == j, 0.0, bot) - factor * pivot
        return bot

    def panel(base, p):
        start = pl.multiple_of(p * PANEL, PANEL)
        slab = mat[:, pl.ds(start, PANEL), :].reshape(regions * PANEL, MEMBERS)
        slab = pltpu.roll(slab, lax.rem(MEMBERS - start, MEMBERS), 1).reshape(regions, PANEL, MEMBERS)
        top = eliminate(slab[:, :HALF], 0)
        bot = jnp.stack([below(top[g], slab[g, HALF:]) for g in range(regions)])
        bot = eliminate(bot, HALF)
        slab = jnp.concatenate([top, bot], axis=1)
        slab = pltpu.roll(slab.reshape(regions * PANEL, MEMBERS), start, 1).reshape(regions, PANEL, MEMBERS)
        mat[:, pl.ds(start, PANEL), :] = slab
        later = p_lane >= start + PANEL
        strict = (p_lane < start + PANEL) & (p_lane - start > p_row)
        clear = (row[base:] >= start + PANEL) & (col[base:] >= start) & (col[base:] < start + PANEL)
        zeros = jnp.zeros((4 * PANEL, MEMBERS), BF16)
        for g in range(0, regions, 2):
            left, right = [], []
            for h in (g, g + 1):
                full = jnp.where(strict, 0.0, slab[h])
                full_h = full.astype(BF16).astype(F32)
                full_l = full - full_h
                factor_h = jnp.where(later, full_h, 0.0)
                factor_l = jnp.where(later, full_l, 0.0)
                left += [factor_h, factor_h, factor_l, factor_l]
                right.append(jnp.concatenate([full_h, full_l, full_h, full_l], axis=0).astype(BF16))
            turned = jnp.concatenate(left, axis=0).T[base:].astype(BF16)
            blocks = jnp.concatenate(
                [
                    jnp.concatenate([right[0], zeros], axis=1),
                    jnp.concatenate([zeros, right[1]], axis=1),
                ],
                axis=0,
            )
            update = jnp.dot(turned, blocks, preferred_element_type=F32)
            mat[g, base:] = jnp.where(clear, 0.0, mat[g, base:]) - update[:, :MEMBERS]
            mat[g + 1, base:] = jnp.where(clear, 0.0, mat[g + 1, base:]) - update[:, MEMBERS:]

    steps = MEMBERS // PANEL
    parts = 4
    for part in range(parts):
        first, last = part * steps // parts, (part + 1) * steps // parts
        each(first, last, functools.partial(panel, first * PANEL))

    means = pmt[...]

    def update_of(g):
        inverse = jnp.where(row >= col, mat[g], 0.0)
        step = jnp.sum(inverse * proj[g, 0:1, :], axis=1, keepdims=True)
        mean_weight = jnp.sum(inverse * step, axis=0, keepdims=True)
        transform = (mean_weight + (MEMBERS - 1.0) ** 0.5 * inverse).astype(BF16)
        pick = (col == g) | (col == regions + g) | (col == 2 * regions + g)
        ones = jnp.where(pick, 1.0, 0.0).astype(BF16)
        return jnp.concatenate([transform, ones], axis=1)

    def apply(s):
        for i in range(BATCH):
            fetch(s * BATCH + i).wait()
        weights = [update_of(s * BATCH + i) for i in range(BATCH)]
        for i in range(BATCH):
            moved = lax.dot_general(
                jnp.concatenate([parbuf[s * BATCH + i], means], axis=1),
                weights[i],
                (((1,), (1,)), ((), ())),
                preferred_element_type=F32,
            )
            outbuf[s * BATCH + i] = moved.astype(BF16)
        for i in range(BATCH):
            put(s * BATCH + i).start()

    each(0, regions // BATCH, apply)
    each(0, regions, lambda g: put(g).wait())


def body(n_region, obs_anomaly, innovation, obs_count, neighbour, taper, param_anomaly, param_mean):
    regions, slots, _ = obs_anomaly.shape
    pars = param_anomaly.shape[1]
    pairs = regions // 2
    vmem = pl.BlockSpec(memory_space=pltpu.VMEM)
    smem = pl.BlockSpec(memory_space=pltpu.SMEM)
    hbm = pl.BlockSpec(memory_space=pltpu.HBM)
    gath = pl.pallas_call(
        functools.partial(gram_kernel, n_region),
        out_shape=jax.ShapeDtypeStruct((3 * pairs, ROWS, MEMBERS), BF16),
        in_specs=[hbm, vmem, smem],
        out_specs=vmem,
        scratch_shapes=[
            pltpu.VMEM((pairs, 2, slots, MEMBERS), BF16),
            pltpu.VMEM((regions, slots), F32),
            pltpu.VMEM((pairs, ROWS, MEMBERS), BF16),
            pltpu.VMEM((pairs, ROWS, MEMBERS), BF16),
        ]
        + [pltpu.SemaphoreType.DMA((pairs,))] * 7,
        compiler_params=pltpu.CompilerParams(
            collective_id=0, has_side_effects=True, vmem_limit_bytes=60 * 2**20
        ),
    )(obs_anomaly, innovation, obs_count)

    return pl.pallas_call(
        functools.partial(solve_kernel, regions * n_region),
        out_shape=jax.ShapeDtypeStruct((regions, pars, MEMBERS), BF16),
        in_specs=[smem, smem, vmem, hbm, vmem],
        out_specs=hbm,
        scratch_shapes=[
            pltpu.VMEM((regions, MEMBERS, MEMBERS), F32),
            pltpu.VMEM((regions, 8, MEMBERS), F32),
            pltpu.VMEM((pars, MEMBERS), BF16),
            pltpu.VMEM((regions, pars, MEMBERS), BF16),
            pltpu.VMEM((regions, pars, MEMBERS), BF16),
            pltpu.SemaphoreType.DMA((regions,)),
            pltpu.SemaphoreType.DMA((regions,)),
        ],
        compiler_params=pltpu.CompilerParams(vmem_limit_bytes=60 * 2**20),
    )(neighbour.T, taper.T, gath, param_anomaly, param_mean)


def solution(mesh):
    in_specs = (
        P("region", "obs", None),
        P("region", "obs"),
        P("region"),
        P("region", None),
        P("region", None),
        P("region", "obs", None),
        P("region", "obs"),
    )
    out_specs = P("region", "obs", None)
    return jax.shard_map(
        functools.partial(body, mesh.shape["region"]),
        mesh=mesh, in_specs=in_specs, out_specs=out_specs, check_vma=False,
    )
```
